512 devices in a mesh: pipe: 2 (over core), dp: 16 (over y, x), tensor: 16 (over z).
Axes of the slice: x: 4, y: 4, z: 16, core: 2. Of those that a mesh axis runs over, the one named last changes fastest.
Arguments:
- x_act: bfloat16 [2, 6144, 16384], P('pipe', 'dp', 'tensor'), may hold values from -6 to 6
- grad_z: bfloat16 [2, 6144, 26624], P('pipe', 'dp', 'tensor'), may hold values from -6 to 6
- weight_tiles: bfloat16 [2, 256, 128, 128], P('pipe', 'tensor'), may hold values from -0.5 to 0.5
- tile_rows: int32 [2, 256], P('pipe', 'tensor'), may hold values from 0 to 127, as said below
- tile_cols: int32 [2, 256], P('pipe', 'tensor'), may hold values from 0 to 12
- err_in: float32 [2, 16, 256, 128, 128], P('pipe', 'dp', 'tensor'), may hold values from -0.3 to 0.3
- kept_mask: int32 [2, 16, 256], P('pipe', 'dp', 'tensor'), may hold values 0 or 1
- tile_list: int32 [2, 16, 192], P('pipe', 'dp', 'tensor'), may hold values from 0 to 23, as said below
- live_count: int32 [2, 16, 16], P('pipe', 'dp', 'tensor'), may hold values from 1 to 12, as said below
Outputs:
- recv_tiles: bfloat16 [2, 16, 192, 128, 128], P('pipe', 'dp', 'tensor')
- err_out: float32 [2, 16, 256, 128, 128], P('pipe', 'dp', 'tensor')
- grad_sum: float32 [2, 16, 16, 128, 128], P('pipe', 'dp', 'tensor')
The draws below stay inside these ranges and needn't reach their ends.
Inputs may be any that keep to these rules, and one draw needn't show every extreme that they name: `tile_rows`: entry j of a tensor rank's 16 entries of one section names a column block held by tensor rank j // (16 / 16), that is one of the blocks ((j // (16 / 16)) * L to that plus L - 1, L = 16384 / (128 * 16)). `tile_list`: A device's 12 entries are distinct tile numbers m * L + b of its own region (L = 16384 / (128 * 16), m < 3, b < L). `live_count`: some device uses all 12 entries of its list.
All inputs are finite; a program needn't handle non-finite values. No bound on the sum of `kept_mask` on one device may be relied on, other than what follows from the above.
Results may differ from the reference program's by a relative error of at most 0.0048.
Values may be sent and summed in bfloat16 or wider, within the bound.
A program may use at most 128 MiB of HBM per device.

```python
import jax
import jax.numpy as jnp
from jax import lax

D = 16384
FF = 26624
BLK = 128
K = 16
TOK = 384
TOKENS = 6144
KSLOT = 1
CAPA = 12
N_PIPE = 2
N_DP = 16
N_TENSOR = 16


def draw_tile_rows(key, part):
    per_owner = K // N_TENSOR
    local_blocks = D // BLK // N_TENSOR
    position = jnp.arange(N_TENSOR * K, dtype=jnp.int32) % K
    owner = position // per_owner
    offset = jax.random.randint(key, (N_PIPE, N_TENSOR * K), 0, local_blocks, dtype=jnp.int32)
    offset = offset.at[0, 0].set(0).at[0, N_TENSOR * K - 1].set(local_blocks - 1)
    return (owner[None, :] * local_blocks + offset).astype(jnp.int32)


def draw_tile_list(key, part):
    region = TOK // BLK * (D // BLK // N_TENSOR)
    capacity = region // 2
    subkeys = jax.random.split(key, N_PIPE * N_DP * N_TENSOR)

    def pick_list(subkey):
        return jax.random.permutation(subkey, region)[:capacity]
    lists = jax.vmap(pick_list)(subkeys)
    return lists.reshape(N_PIPE, N_DP, N_TENSOR * capacity).astype(jnp.int32)


def draw_live_count(key, part):
    region = TOK // BLK * (D // BLK // N_TENSOR)
    capacity = region // 2
    devices_all = N_PIPE * N_DP * N_TENSOR
    counts = jax.random.randint(key, (devices_all,), max(1, capacity // 3), capacity + 1, dtype=jnp.int32)
    chosen = jax.random.randint(jax.random.fold_in(key, 7), (), 0, devices_all, dtype=jnp.int32)
    counts = jnp.where(jnp.arange(devices_all, dtype=jnp.int32) == chosen, capacity, counts)
    return counts.reshape(N_PIPE, N_DP, N_TENSOR).astype(jnp.int32)


def plant(result, key, smallest, high):
    spot = [jax.random.randint(jax.random.fold_in(key, axis), (), 0, length) for axis, length in enumerate(result.shape)]
    widest = result.shape.index(max(result.shape))
    beside = spot[:widest] + [(spot[widest] + 1) % result.shape[widest]] + spot[widest + 1:]
    return result.at[tuple(spot)].set(smallest).at[tuple(beside)].set(high)


def strengthened(drawn, stream_key, source, target, parts, factor):
    def block_of(dim):
        return (jnp.arange(drawn.shape[dim]) // (drawn.shape[dim] // parts)).reshape((-1,) + (1,) * (drawn.ndim - 1 - dim))

    one_side = jax.random.permutation(stream_key, parts)[block_of(target)]
    second = (block_of(target) + parts // 2) % parts
    return jnp.where((block_of(source) == one_side) | (block_of(source) == second), factor * drawn, drawn)


def level_of(key, dims, pieces, smallest, high):
    def one(dim, parts):
        heights = jax.random.uniform(jax.random.fold_in(jax.random.fold_in(key, 6), dim), (parts,), jnp.float32, smallest / len(pieces), high / len(pieces))
        return jnp.repeat(jnp.exp(heights), dims[dim] // parts).reshape((-1,) + (1,) * (len(dims) - dim - 1))

    factor_of = one(*pieces[0])
    for cut in pieces[1:]:
        factor_of = factor_of * one(*cut)
    return factor_of


def centred(own_key, extent, scale, most, cuts=(), held_as=jnp.bfloat16):
    factor_of = level_of(own_key, extent, cuts, -0.22, 0.18) if cuts else 1.0
    entries = jax.random.normal(own_key, extent, jnp.float32) * scale * factor_of
    return jnp.minimum(jnp.maximum(entries, -most), most).astype(held_as)


def heavy_noise(stream_key, shape, spread, reach, shards, heavy, kind=jnp.bfloat16):
    drawn = spread * jax.random.normal(stream_key, shape, jnp.float32)
    if shards:
        drawn = drawn * level_of(stream_key, shape, shards, -0.22, 0.18)
    return jnp.clip(strengthened(drawn, jax.random.fold_in(stream_key, 3), *heavy), -reach, reach).astype(kind)


def setup_inputs(seed: int = 0) -> dict:
    splits = jax.random.split(jax.random.key(seed), 10)
    return {
        "x_act": centred(splits[0], (N_PIPE, TOKENS, D), 1.0, 6.0, ((0, 2), (1, 16), (2, 16))),
        "grad_z": centred(splits[1], (N_PIPE, TOKENS, FF), 1.0, 6.0, ((0, 2), (1, 16), (2, 16))),
        "weight_tiles": centred(splits[2], (N_PIPE, N_TENSOR * K, BLK, BLK), BLK ** -0.5, 0.5, ((0, 2), (1, 16))),
        "tile_rows": draw_tile_rows(jax.random.fold_in(splits[9], 71), 0),
        "tile_cols": plant(jax.random.randint(splits[4], (N_PIPE, N_TENSOR * K), 0, FF // BLK // N_TENSOR), jax.random.fold_in(splits[4], 1), 0, (FF // BLK // N_TENSOR) - 1).astype(jnp.int32),
        "err_in": heavy_noise(splits[5], (N_PIPE, N_DP, N_TENSOR * K, BLK, BLK), 0.05, 0.3, ((0, 2), (1, 16), (2, 16)), (1, 2, 16, 2.0), jnp.float32),
        "kept_mask": plant((jax.random.randint(splits[6], (N_PIPE, N_DP, N_TENSOR * K), 0, 2) < 1).astype(jnp.int32), jax.random.fold_in(splits[6], 1), 0, 1),
        "tile_list": draw_tile_list(jax.random.fold_in(splits[9], 71), 0),
        "live_count": draw_live_count(jax.random.fold_in(splits[9], 71), 0),
    }


def reference(x_act, grad_z, weight_tiles, tile_rows, tile_cols, err_in, kept_mask, tile_list, live_count):
    col_blocks = D // BLK
    local_blocks = col_blocks // N_TENSOR
    ff_local = FF // BLK // N_TENSOR
    tok_blocks = TOK // BLK
    tile_total = N_TENSOR * K
    tile_index = jnp.arange(tile_total, dtype=jnp.int32)
    owner_index = jnp.arange(N_TENSOR, dtype=jnp.int32)
    slot_index = jnp.arange(CAPA, dtype=jnp.int32)

    def one_pair(pair):
        section = pair // N_DP
        member = pair % N_DP
        inputs = lax.dynamic_slice_in_dim(x_act[section], (member * TOK).astype(jnp.int32), TOK, 0)
        grads_out = lax.dynamic_slice_in_dim(grad_z[section], (member * TOK).astype(jnp.int32), TOK, 0)
        row_ids = tile_rows[section]
        col_ids = (tile_index // K) * ff_local + tile_cols[section]
        input_sel = jnp.take(inputs.reshape(TOK, col_blocks, BLK), row_ids, axis=1)
        grad_sel = jnp.take(grads_out.reshape(TOK, N_TENSOR * ff_local, BLK), col_ids, axis=1)
        weight_grads = jnp.einsum('tgc,tgf->gcf', input_sel.astype(jnp.float32), grad_sel.astype(jnp.float32)) * (1.0 / TOK)
        accumulated = weight_grads + err_in[section, member]
        keep_now = (kept_mask[section, member] == 1)[:, None, None]
        sent_tiles = jnp.where(keep_now, accumulated, jnp.float32(0.0))
        residual = accumulated - sent_tiles
        partial_value = jnp.einsum('tgf,gcf->gtc', grad_sel.astype(jnp.float32), weight_tiles[section].astype(jnp.float32))
        partial_value = lax.optimization_barrier(partial_value.astype(jnp.bfloat16)).astype(jnp.float32)
        input_grad = jax.ops.segment_sum(partial_value, row_ids, num_segments=col_blocks).astype(jnp.bfloat16)
        grid = input_grad.reshape(N_TENSOR, local_blocks, tok_blocks, BLK, BLK)
        listed = tile_list[section, member].reshape(N_TENSOR, CAPA)
        picked = grid[owner_index[:, None], listed % local_blocks, listed // local_blocks]
        valid = slot_index[None, :] < live_count[section, member][:, None]
        picked = jnp.where(valid[:, :, None, None], picked, jnp.zeros_like(picked))
        return residual, sent_tiles, picked.reshape(N_TENSOR * CAPA, BLK, BLK)

    residual, sent_tiles, packed = lax.map(one_pair, jnp.arange(N_PIPE * N_DP, dtype=jnp.int32))
    err_out = residual.reshape(N_PIPE, N_DP, tile_total, BLK, BLK)
    totals = jnp.sum(sent_tiles.reshape(N_PIPE, N_DP, tile_total, BLK, BLK), axis=1)
    grad_sum = totals.reshape(N_PIPE, N_TENSOR, N_DP, KSLOT, BLK, BLK).transpose(0, 2, 1, 3, 4, 5)
    grad_sum = grad_sum.reshape(N_PIPE, N_DP, N_TENSOR * KSLOT, BLK, BLK)
    packed = packed.reshape(N_PIPE, N_DP, N_TENSOR * CAPA, BLK, BLK)
    recv_tiles = jnp.roll(packed, -1, axis=0)
    return recv_tiles, err_out, grad_sum
```

```python
import functools

import jax
import jax.numpy as jnp
from jax import lax
from jax.experimental import pallas as pl
from jax.experimental.pallas import tpu as pltpu
from jax.sharding import PartitionSpec as P

MESH = pl.DeviceIdType.MESH
WINDOW = 4
LAG = 2
BF16, F32 = jnp.bfloat16, jnp.float32


def kernel(
    n, n_dp, x_hbm, z_hbm, w_hbm, err_hbm, rows_s, cols_s, mask_s, list_s, live_s,
    recv_o, err_o, sum_o,
    xv, zv, errv, zsend, zrecv, wz, wfull, idx_out, idx_in, idx_s, gsend, grecv, eout, sbuf, sumr, sumv, part, acc, packed,
    zl_sem, xl_sem, load_sem, ix_s, ix_r, ws_s, ws_r, wb_s, wb_r, zs_s, zs_r, gr_s, gr_r, dp_s, dp_r, pp_s, pp_r, eo_s, misc,
):
    tok, blk = zsend.shape[1], zsend.shape[2]
    rounds = n - 1
    local_blocks, hidden_blocks = xv.shape[0], zv.shape[0]
    slots = acc.shape[0]
    chunks, chunk_rows = wfull.shape[2], wfull.shape[3]
    p, d, t = lax.axis_index("pipe"), lax.axis_index("dp"), lax.axis_index("tensor")
    part_of, half = lax.rem(d, chunks), lax.div(d, chunks)
    halves = n_dp // chunks

    def offset(k):
        q = k + 1
        dist = n // 2 - lax.div(q, 2)
        return dist + (1 - lax.rem(q, 2)) * (n - 2 * dist)

    def to_of(k):
        return lax.rem(t + offset(k), n)

    def from_of(k):
        return lax.rem(t + n - offset(k), n)

    def remote(src, dst, s_sem, r_sem, where):
        return pltpu.make_async_remote_copy(
            src_ref=src, dst_ref=dst, send_sem=s_sem, recv_sem=r_sem, device_id=where, device_id_type=MESH
        )

    def z_copy(k):
        return remote(zsend.at[k], zrecv.at[k], zs_s.at[k], zs_r.at[k], {"tensor": to_of(k)})

    def idx_copy(k):
        return remote(idx_out, idx_in.at[k], ix_s.at[k], ix_r.at[k], {"tensor": to_of(k)})

    def w_copy(k):
        src = w_hbm.at[0, to_of(k), pl.ds(pl.multiple_of(part_of * chunk_rows, chunk_rows), chunk_rows)]
        return remote(src, wz.at[lax.div(t, halves), lax.rem(t, halves)], ws_s.at[k], ws_r.at[k], {"tensor": to_of(k)})

    def w_share(i):
        return remote(
            wz.at[:, half], wfull.at[:, half, part_of], wb_s.at[i], wb_r.at[i], {"dp": lax.rem(d + i + 1, n_dp)}
        )

    def g_copy(k):
        return remote(gsend.at[k], grecv.at[k], gr_s.at[k], gr_r.at[k], {"tensor": from_of(k)})

    z_loads = [
        pltpu.make_async_copy(z_hbm.at[0, :, pl.ds(i * blk, blk)], zv.at[i], zl_sem.at[i])
        for i in range(hidden_blocks)
    ]
    x_loads = [
        pltpu.make_async_copy(x_hbm.at[0, :, pl.ds(i * blk, blk)], xv.at[i], xl_sem.at[i])
        for i in range(local_blocks)
    ]
    err_load = pltpu.make_async_copy(err_hbm.at[0, 0], errv, load_sem.at[0])
    for load in (*z_loads, *x_loads, err_load):
        load.start()
    own_w = pltpu.make_async_copy(
        w_hbm.at[0, t, pl.ds(pl.multiple_of(part_of * chunk_rows, chunk_rows), chunk_rows)],
        wz.at[lax.div(t, halves), lax.rem(t, halves)],
        load_sem.at[1],
    )
    own_w.start()

    barrier = pltpu.get_barrier_semaphore()

    def greet_z(i, carry):
        pl.semaphore_signal(barrier, inc=1, device_id={"tensor": lax.rem(t + i, n)}, device_id_type=MESH)
        return carry

    def greet_dp(i, carry):
        pl.semaphore_signal(barrier, inc=1, device_id={"dp": lax.rem(d + i, n_dp)}, device_id_type=MESH)
        return carry

    lax.fori_loop(1, n, greet_z, 0)
    lax.fori_loop(1, n_dp, greet_dp, 0)
    pl.semaphore_signal(barrier, inc=1, device_id={"pipe": 1 - p}, device_id_type=MESH)

    lane = lax.broadcasted_iota(jnp.int32, idx_out.shape, 1)
    row = jnp.zeros(idx_out.shape, jnp.int32)
    for j in range(n):
        row = jnp.where(lane == j, rows_s[0, j], row)
    idx_out[...] = row

    def z_block(j):
        return zv[cols_s[0, j]]

    for load in z_loads:
        load.wait()

    def pick(k, carry):
        zsend[k] = z_block(to_of(k))
        return carry

    lax.fori_loop(0, rounds, pick, 0)

    pl.semaphore_wait(barrier, n - 1 + n_dp - 1 + 1)

    def small(k, carry):
        idx_copy(k).start()
        w_copy(k).start()
        return carry

    lax.fori_loop(0, rounds, small, 0)

    def start_z(k, carry):
        z_copy(k).start()
        return carry

    lax.fori_loop(0, min(WINDOW, rounds), start_z, 0)

    def weight_grad(zblk, b):
        g = lax.dot_general(xv[b], zblk, (((0,), (0,)), ((), ())), preferred_element_type=F32)
        return g * (1.0 / tok)

    def add_terms(zblk, src, b):
        w = wfull[lax.div(src, halves), lax.rem(src, halves)].reshape(blk, blk)
        product = lax.dot_general(zblk, w, (((1,), (1,)), ((), ())), preferred_element_type=F32)
        part[...] = product.astype(BF16).reshape(part.shape)
        for s in range(slots):
            r = list_s[0, 0, s]
            m = lax.div(r, local_blocks)
            term = part[m].astype(F32)
            miss = jnp.full((blk, blk), r - m * local_blocks - b, jnp.int32)
            acc[s] = acc[s] + jnp.where(miss == 0, term, 0.0)

    def dp_copy(slot, j):
        return remote(sbuf.at[slot], sumr.at[d], dp_s.at[slot], dp_r.at[d], {"dp": j})

    def err_copy(j):
        return pltpu.make_async_copy(eout.at[j], err_o.at[0, 0, j], eo_s.at[j])

    def feedback(slot, j, grads):
        total = grads + errv[j]
        keep = jnp.full((blk, blk), mask_s[0, 0, j], jnp.int32) == 1
        eout[j] = jnp.where(keep, 0.0, total)
        err_copy(j).start()
        sent = jnp.where(keep, total, 0.0).astype(BF16)
        sbuf[slot] = sent

        @pl.when(j != d)
        def _():
            dp_copy(slot, j).start()

        @pl.when(j == d)
        def _():
            sumr[d] = sent

    for load in (*x_loads, err_load):
        load.wait()
    for s in range(slots):
        acc[s] = jnp.zeros((blk, blk), F32)
    feedback(rounds, t, weight_grad(z_block(t), lax.rem(rows_s[0, t], local_blocks)))

    def got_idx(k, carry):
        idx_copy(k).wait_recv()
        return carry

    lax.fori_loop(0, rounds, got_idx, 0)
    to_smem = pltpu.make_async_copy(idx_in, idx_s, misc.at[0])
    to_smem.start()

    def got_w(k, carry):
        w_copy(k).wait_recv()
        return carry

    lax.fori_loop(0, rounds, got_w, 0)
    own_w.wait()
    keep_w = pltpu.make_async_copy(wz.at[:, half], wfull.at[:, half, part_of], misc.at[1])
    keep_w.start()

    def share(i, carry):
        w_share(i).start()
        return carry

    lax.fori_loop(0, n_dp - 1, share, 0)
    to_smem.wait()
    keep_w.wait()

    def got_share(i, carry):
        w_share(i).wait_recv()
        return carry
        return carry

    def returned(k):
        g_copy(k).wait_recv()
        feedback(k, to_of(k), grecv[k].astype(F32))

    def one_round(k, carry):
        z_copy(k).wait_recv()

        @pl.when(k + WINDOW < rounds)
        def _():
            z_copy(k + WINDOW).start()

        zblk = zrecv[k]
        b = lax.rem(idx_s[k, 0, t], local_blocks)
        gsend[k] = weight_grad(zblk, b).astype(BF16)
        g_copy(k).start()

        @pl.when(k == 0)
        def _():
            lax.fori_loop(0, n_dp - 1, got_share, 0)

        add_terms(zblk, from_of(k), b)

        @pl.when(k >= LAG)
        def _():
            returned(k - LAG)

        return carry

    lax.fori_loop(0, rounds, one_round, 0)
    add_terms(z_block(t), t, lax.rem(rows_s[0, t], local_blocks))
    live = live_s[0, 0, 0]
    for s in range(slots):
        packed[s] = jnp.where(jnp.full((blk, blk), live, jnp.int32) > s, acc[s], 0.0).astype(BF16)
    over = remote(packed, recv_o.at[0, 0], pp_s.at[0], pp_r.at[0], {"pipe": 1 - p})
    over.start()
    for k in range(rounds - LAG, rounds):
        returned(k)

    def dp_in(i, total):
        src = lax.rem(d + i, n_dp)
        remote(sbuf.at[0], sumr.at[src], dp_s.at[0], dp_r.at[src], {"dp": src}).wait_recv()
        return total + sumr[src].astype(F32)

    sumv[...] = lax.fori_loop(1, n_dp, dp_in, sumr[d].astype(F32))
    out = pltpu.make_async_copy(sumv, sum_o.at[0, 0, 0], misc.at[2])
    out.start()

    def drain(k, carry):
        z_copy(k).wait_send()
        idx_copy(k).wait_send()
        w_copy(k).wait_send()
        g_copy(k).wait_send()
        err_copy(k).wait()

        @pl.when(to_of(k) != d)
        def _():
            dp_copy(k, to_of(k)).wait_send()

        return carry

    lax.fori_loop(0, rounds, drain, 0)
    err_copy(rounds).wait()

    @pl.when(t != d)
    def _():
        dp_copy(rounds, t).wait_send()

    def drain_share(i, carry):
        w_share(i).wait_send()
        return carry

    lax.fori_loop(0, n_dp - 1, drain_share, 0)
    over.wait()
    out.wait()


def local(n, n_dp, x_act, grad_z, weight_tiles, tile_rows, tile_cols, err_in, kept_mask, tile_list, live_count):
    tok, width = x_act.shape[1], x_act.shape[2]
    hidden = grad_z.shape[2]
    blk = weight_tiles.shape[2]
    slots = tile_list.shape[2]
    rounds = n - 1
    chunks = min(8, n_dp)
    rows = blk // chunks
    halves = n_dp // chunks
    dma = pltpu.SemaphoreType.DMA
    hbm = pl.BlockSpec(memory_space=pl.ANY)
    smem = pl.BlockSpec(memory_space=pltpu.SMEM)
    return pl.pallas_call(
        functools.partial(kernel, n, n_dp),
        out_shape=(
            jax.ShapeDtypeStruct((1, 1, slots, blk, blk), BF16),
            jax.ShapeDtypeStruct((1, 1, n, blk, blk), F32),
            jax.ShapeDtypeStruct((1, 1, 1, blk, blk), F32),
        ),
        in_specs=[hbm] * 4 + [smem] * 5,
        out_specs=(hbm, hbm, hbm),
        scratch_shapes=[
            pltpu.VMEM((width // blk, tok, blk), BF16),
            pltpu.VMEM((hidden // blk, tok, blk), BF16),
            pltpu.VMEM((n, blk, blk), F32),
            pltpu.VMEM((rounds, tok, blk), BF16),
            pltpu.VMEM((rounds, tok, blk), BF16),
            pltpu.VMEM((n // halves, halves, rows, blk), BF16),
            pltpu.VMEM((n // halves, halves, chunks, rows, blk), BF16),
            pltpu.VMEM((1, blk), jnp.int32),
            pltpu.VMEM((rounds, 1, blk), jnp.int32),
            pltpu.SMEM((rounds, 1, blk), jnp.int32),
            pltpu.VMEM((rounds, blk, blk), BF16),
            pltpu.VMEM((rounds, blk, blk), BF16),
            pltpu.VMEM((n, blk, blk), F32),
            pltpu.VMEM((n, blk, blk), BF16),
            pltpu.VMEM((n_dp, blk, blk), BF16),
            pltpu.VMEM((blk, blk), F32),
            pltpu.VMEM((tok // blk, blk, blk), BF16),
            pltpu.VMEM((slots, blk, blk), F32),
            pltpu.VMEM((slots, blk, blk), BF16),
            dma((hidden // blk,)), dma((width // blk,)), dma((2,)),
            dma((rounds,)), dma((rounds,)),
            dma((rounds,)), dma((rounds,)),
            dma((n_dp - 1,)), dma((n_dp - 1,)),
            dma((rounds,)), dma((rounds,)),
            dma((rounds,)), dma((rounds,)),
            dma((n,)), dma((n_dp,)),
            dma((1,)), dma((1,)),
            dma((n,)),
            dma((3,)),
        ],
        compiler_params=pltpu.CompilerParams(
            collective_id=0, has_side_effects=True, vmem_limit_bytes=40 * 2**20
        ),
        cost_estimate=pl.CostEstimate(flops=10**9, bytes_accessed=5 * 10**6, transcendentals=0),
    )(x_act, grad_z, weight_tiles, err_in, tile_rows, tile_cols, kept_mask, tile_list, live_count)


def solution(mesh):
    n, n_dp = mesh.shape["tensor"], mesh.shape["dp"]
    return jax.shard_map(
        functools.partial(local, n, n_dp),
        mesh=mesh,
        in_specs=(
            P("pipe", "dp", "tensor"),
            P("pipe", "dp", "tensor"),
            P("pipe", "tensor", None, None),
            P("pipe", "tensor"),
            P("pipe", "tensor"),
            P("pipe", "dp", "tensor", None, None),
            P("pipe", "dp", "tensor"),
            P("pipe", "dp", "tensor"),
            P("pipe", "dp", "tensor"),
        ),
        out_specs=(
            P("pipe", "dp", "tensor", None, None),
            P("pipe", "dp", "tensor", None, None),
            P("pipe", "dp", "tensor", None, None),
        ),
        check_vma=False,
    )
```

```python
import functools

import jax
import jax.numpy as jnp
from jax import lax
from jax.experimental import pallas as pl
from jax.experimental.pallas import tpu as pltpu
from jax.sharding import PartitionSpec as P

MESH = pl.DeviceIdType.MESH
WINDOW = 4
LAG = 3
TERM_LAG = 3
BF16, F32 = jnp.bfloat16, jnp.float32


def kernel(
    n, n_dp, x_hbm, z_hbm, w_hbm, err_hbm, cols_h, rows_h, mask_h, list_h, live_h,
    recv_o, err_o, sum_o,
    cols_s, rows_s, mask_s, list_s, live_s, xv, zv, errv, zsend, zrecv, wz, wfull, idx_out, idx_in, idx_s, gsend, grecv, eout, sbuf, sumr, sumv, part, acc, packed,
    int_sem, zl_sem, xl_sem, load_sem, ix_s, ix_r, ws_s, ws_r, wb_s, wb_r, zs_s, zs_r, gr_s, gr_r, dp_s, dp_r, pp_s, pp_r, eo_s, misc,
):
    tok, blk = zsend.shape[1], zsend.shape[2]
    rounds = n - 1
    term_lag = min(TERM_LAG, rounds - 1)
    local_blocks, hidden_blocks = xv.shape[0], zv.shape[0]
    slots = acc.shape[0]
    chunks, chunk_rows = wfull.shape[2], wfull.shape[3]
    p, d, t = lax.axis_index("pipe"), lax.axis_index("dp"), lax.axis_index("tensor")
    part_of, half = lax.rem(d, chunks), lax.div(d, chunks)
    halves = n_dp // chunks

    def offset(k):
        q = lax.rem(k + rounds - 2, rounds) + 1
        dist = n // 2 - lax.div(q, 2)
        return dist + (1 - lax.rem(q, 2)) * (n - 2 * dist)

    def carries(rank):
        return lax.rem(rank, halves) == half

    def to_of(k):
        return lax.rem(t + offset(k), n)

    def from_of(k):
        return lax.rem(t + n - offset(k), n)

    def remote(src, dst, s_sem, r_sem, where):
        return pltpu.make_async_remote_copy(
            src_ref=src, dst_ref=dst, send_sem=s_sem, recv_sem=r_sem, device_id=where, device_id_type=MESH
        )

    def z_copy(k):
        return remote(zsend.at[k], zrecv.at[k], zs_s.at[k], zs_r.at[k], {"tensor": to_of(k)})

    def idx_copy(k):
        return remote(idx_out, idx_in.at[k], ix_s.at[k], ix_r.at[k], {"tensor": to_of(k)})

    def w_copy(k):
        src = w_hbm.at[0, to_of(k), pl.ds(pl.multiple_of(part_of * chunk_rows, chunk_rows), chunk_rows)]
        return remote(src, wz.at[lax.div(t, halves)], ws_s.at[k], ws_r.at[k], {"tensor": to_of(k)})

    def w_share(i):
        return remote(
            wz, wfull.at[:, half, part_of], wb_s.at[i], wb_r.at[i], {"dp": lax.rem(d + i + 1, n_dp)}
        )

    def g_copy(k):
        return remote(gsend.at[k], grecv.at[k], gr_s.at[k], gr_r.at[k], {"tensor": from_of(k)})

    barrier = pltpu.get_barrier_semaphore()

    def greet_z(i, carry):
        pl.semaphore_signal(barrier, inc=1, device_id={"tensor": lax.rem(t + i, n)}, device_id_type=MESH)
        return carry

    def greet_dp(i, carry):
        pl.semaphore_signal(barrier, inc=1, device_id={"dp": lax.rem(d + i, n_dp)}, device_id_type=MESH)
        return carry

    lax.fori_loop(1, n, greet_z, 0)
    lax.fori_loop(1, n_dp, greet_dp, 0)
    pl.semaphore_signal(barrier, inc=1, device_id={"pipe": 1 - p}, device_id_type=MESH)

    int_loads = [
        pltpu.make_async_copy(src, dst, int_sem.at[i])
        for i, (src, dst) in enumerate(
            ((cols_h, cols_s), (rows_h, rows_s), (mask_h, mask_s), (list_h, list_s), (live_h, live_s))
        )
    ]
    for load in int_loads:
        load.start()
    z_loads = [
        pltpu.make_async_copy(z_hbm.at[0, :, pl.ds(i * blk, blk)], zv.at[i], zl_sem.at[i])
        for i in range(hidden_blocks)
    ]
    x_loads = [
        pltpu.make_async_copy(x_hbm.at[0, :, pl.ds(i * blk, blk)], xv.at[i], xl_sem.at[i])
        for i in range(local_blocks)
    ]
    err_load = pltpu.make_async_copy(err_hbm.at[0, 0], errv, load_sem.at[0])
    for load in z_loads:
        load.start()
    for load in int_loads:
        load.wait()
    lane = lax.broadcasted_iota(jnp.int32, idx_out.shape, 1)
    row = jnp.zeros(idx_out.shape, jnp.int32)
    for j in range(n):
        row = jnp.where(lane == j, rows_s[0, j], row)
    idx_out[...] = row

    def z_block(j):
        return zv[cols_s[0, j]]

    for load in z_loads:
        load.wait()

    def pick(k, carry):
        zsend[k] = z_block(to_of(k))
        return carry

    lax.fori_loop(0, min(WINDOW, rounds), pick, 0)

    own_w = pltpu.make_async_copy(
        w_hbm.at[0, t, pl.ds(pl.multiple_of(part_of * chunk_rows, chunk_rows), chunk_rows)],
        wz.at[lax.div(t, halves)],
        load_sem.at[1],
    )

    @pl.when(carries(t))
    def _():
        own_w.start()
    for load in (*x_loads, err_load):
        load.start()
    pl.semaphore_wait(barrier, n - 1 + n_dp - 1 + 1)

    def small(k, carry):
        idx_copy(k).start()

        @pl.when(carries(t))
        def _():
            w_copy(k).start()

        return carry


    def start_z(k, carry):
        z_copy(k).start()
        return carry

    lax.fori_loop(0, rounds, small, 0)
    lax.fori_loop(0, min(WINDOW, rounds), start_z, 0)
    lax.fori_loop(min(WINDOW, rounds), rounds, pick, 0)

    def weight_grad(zblk, b):
        g = lax.dot_general(xv[b], zblk, (((0,), (0,)), ((), ())), preferred_element_type=F32)
        return g * (1.0 / tok)

    def add_terms(zblk, src, b):
        w = wfull[lax.div(src, halves), lax.rem(src, halves)].reshape(blk, blk)
        product = lax.dot_general(zblk, w, (((1,), (1,)), ((), ())), preferred_element_type=F32)
        part[...] = product.astype(BF16).reshape(part.shape)
        for s in range(slots):
            r = list_s[0, 0, s]
            m = lax.div(r, local_blocks)
            term = part[m].astype(F32)
            miss = jnp.full((blk, blk), r - m * local_blocks - b, jnp.int32)
            acc[s] = acc[s] + jnp.where(miss == 0, term, 0.0)

    def dp_copy(slot, j):
        return remote(sbuf.at[slot], sumr.at[d], dp_s.at[slot], dp_r.at[d], {"dp": j})

    def err_copy(j):
        return pltpu.make_async_copy(eout.at[j], err_o.at[0, 0, j], eo_s.at[j])

    def feedback(slot, j, grads):
        total = grads + errv[j]
        keep = jnp.full((blk, blk), mask_s[0, 0, j], jnp.int32) == 1
        eout[j] = jnp.where(keep, 0.0, total)
        err_copy(j).start()
        sent = jnp.where(keep, total, 0.0).astype(BF16)
        sbuf[slot] = sent

        @pl.when(j != d)
        def _():
            dp_copy(slot, j).start()

        @pl.when(j == d)
        def _():
            sumr[d] = sent

    for load in (*x_loads, err_load):
        load.wait()
    for s in range(slots):
        acc[s] = jnp.zeros((blk, blk), F32)
    feedback(rounds, t, weight_grad(z_block(t), lax.rem(rows_s[0, t], local_blocks)))

    def got_idx(k, carry):
        idx_copy(k).wait_recv()
        return carry

    lax.fori_loop(0, rounds, got_idx, 0)
    to_smem = pltpu.make_async_copy(idx_in, idx_s, misc.at[0])
    to_smem.start()

    def got_w(k, carry):
        @pl.when(carries(from_of(k)))
        def _():
            w_copy(k).wait_recv()

        return carry

    lax.fori_loop(0, rounds, got_w, 0)

    @pl.when(carries(t))
    def _():
        own_w.wait()

    keep_w = pltpu.make_async_copy(wz, wfull.at[:, half, part_of], misc.at[1])
    keep_w.start()

    def share(i, carry):
        w_share(i).start()
        return carry

    lax.fori_loop(0, n_dp - 1, share, 0)
    to_smem.wait()
    keep_w.wait()

    def got_share(i, carry):
        w_share(i).wait_recv()
        return carry
        return carry

    def returned(k):
        g_copy(k).wait_recv()
        feedback(k, to_of(k), grecv[k].astype(F32))

    def local_of(k):
        return lax.rem(idx_s[k, 0, t], local_blocks)

    def terms(k):
        add_terms(zrecv[k], from_of(k), local_of(k))

    def one_round(k, carry):
        z_copy(k).wait_recv()

        @pl.when(k + WINDOW < rounds)
        def _():
            z_copy(k + WINDOW).start()

        gsend[k] = weight_grad(zrecv[k], local_of(k)).astype(BF16)
        g_copy(k).start()

        @pl.when(k == term_lag)
        def _():
            lax.fori_loop(0, n_dp - 1, got_share, 0)

        @pl.when(k >= term_lag)
        def _():
            terms(k - term_lag)

        @pl.when(k >= LAG)
        def _():
            returned(k - LAG)

        return carry

    lax.fori_loop(0, rounds, one_round, 0)
    lax.fori_loop(rounds - term_lag, rounds, lambda k, carry: (terms(k), carry)[1], 0)
    add_terms(z_block(t), t, lax.rem(rows_s[0, t], local_blocks))
    live = live_s[0, 0, 0]
    for s in range(slots):
        packed[s] = jnp.where(jnp.full((blk, blk), live, jnp.int32) > s, acc[s], 0.0).astype(BF16)
    over = remote(packed, recv_o.at[0, 0], pp_s.at[0], pp_r.at[0], {"pipe": 1 - p})
    over.start()
    for k in range(rounds - LAG, rounds):
        returned(k)

    def drain(k, carry):
        z_copy(k).wait_send()
        idx_copy(k).wait_send()
        g_copy(k).wait_send()

        @pl.when(carries(t))
        def _():
            w_copy(k).wait_send()

        @pl.when(to_of(k) != d)
        def _():
            dp_copy(k, to_of(k)).wait_send()

        return carry

    def drain_share(i, carry):
        w_share(i).wait_send()
        return carry

    lax.fori_loop(0, rounds, drain, 0)
    lax.fori_loop(0, n_dp - 1, drain_share, 0)

    @pl.when(t != d)
    def _():
        dp_copy(rounds, t).wait_send()

    def dp_in(i, total):
        src = lax.rem(d + i, n_dp)
        remote(sbuf.at[0], sumr.at[src], dp_s.at[0], dp_r.at[src], {"dp": src}).wait_recv()
        return total + sumr[src].astype(F32)

    sumv[...] = lax.fori_loop(1, n_dp, dp_in, sumr[d].astype(F32))
    out = pltpu.make_async_copy(sumv, sum_o.at[0, 0, 0], misc.at[2])
    out.start()

    def drain_err(j, carry):
        err_copy(j).wait()
        return carry

    lax.fori_loop(0, n, drain_err, 0)
    over.wait()
    out.wait()


def hand_over(tiles_in, err_in, sum_in, tiles_out, err_out, sum_out, tiles, err, total, sem):
    steps = [(tiles_in, tiles, tiles_out), (sum_in, total, sum_out)]
    steps += [(err_in.at[0, 0, j], err.at[0, 0, j], err_out.at[0, 0, j]) for j in range(err_in.shape[2])]
    arriving = [pltpu.make_async_copy(src, mid, sem.at[0, i]) for i, (src, mid, _) in enumerate(steps)]
    leaving = [pltpu.make_async_copy(mid, dst, sem.at[1, i]) for i, (_, mid, dst) in enumerate(steps)]
    for copy in arriving:
        copy.start()
    for before, after in zip(arriving, leaving):
        before.wait()
        after.start()
    for copy in leaving:
        copy.wait()


def local(n, n_dp, x_act, grad_z, weight_tiles, tile_rows, tile_cols, err_in, kept_mask, tile_list, live_count):
    tok, width = x_act.shape[1], x_act.shape[2]
    hidden = grad_z.shape[2]
    blk = weight_tiles.shape[2]
    slots = tile_list.shape[2]
    rounds = n - 1
    chunks = min(8, n_dp)
    rows = blk // chunks
    halves = n_dp // chunks
    dma = pltpu.SemaphoreType.DMA
    hbm = pl.BlockSpec(memory_space=pl.ANY)
    ints = (tile_cols, tile_rows, kept_mask, tile_list, live_count)
    shapes = (
        jax.ShapeDtypeStruct((1, 1, slots, blk, blk), BF16),
        jax.ShapeDtypeStruct((1, 1, n, blk, blk), F32),
        jax.ShapeDtypeStruct((1, 1, 1, blk, blk), F32),
    )
    results = pl.pallas_call(
        functools.partial(kernel, n, n_dp),
        out_shape=shapes,
        in_specs=[hbm] * 9,
        out_specs=(hbm, hbm, hbm),
        scratch_shapes=[pltpu.SMEM(a.shape, a.dtype) for a in ints]
        + [
            pltpu.VMEM((width // blk, tok, blk), BF16),
            pltpu.VMEM((hidden // blk, tok, blk), BF16),
            pltpu.VMEM((n, blk, blk), F32),
            pltpu.VMEM((rounds, tok, blk), BF16),
            pltpu.VMEM((rounds, tok, blk), BF16),
            pltpu.VMEM((n // halves, rows, blk), BF16),
            pltpu.VMEM((n // halves, halves, chunks, rows, blk), BF16),
            pltpu.VMEM((1, blk), jnp.int32),
            pltpu.VMEM((rounds, 1, blk), jnp.int32),
            pltpu.SMEM((rounds, 1, blk), jnp.int32),
            pltpu.VMEM((rounds, blk, blk), BF16),
            pltpu.VMEM((rounds, blk, blk), BF16),
            pltpu.VMEM((n, blk, blk), F32),
            pltpu.VMEM((n, blk, blk), BF16),
            pltpu.VMEM((n_dp, blk, blk), BF16),
            pltpu.VMEM((blk, blk), F32),
            pltpu.VMEM((tok // blk, blk, blk), BF16),
            pltpu.VMEM((slots, blk, blk), F32),
            pltpu.VMEM((slots, blk, blk), BF16),
            dma((len(ints),)), dma((hidden // blk,)), dma((width // blk,)), dma((2,)),
            dma((rounds,)), dma((rounds,)),
            dma((rounds,)), dma((rounds,)),
            dma((n_dp - 1,)), dma((n_dp - 1,)),
            dma((rounds,)), dma((rounds,)),
            dma((rounds,)), dma((rounds,)),
            dma((n,)), dma((n_dp,)),
            dma((1,)), dma((1,)),
            dma((n,)),
            dma((3,)),
        ],
        compiler_params=pltpu.CompilerParams(
            collective_id=0, has_side_effects=True, vmem_limit_bytes=56 * 2**20
        ),
        cost_estimate=pl.CostEstimate(flops=10**9, bytes_accessed=5 * 10**6, transcendentals=0),
    )(x_act, grad_z, weight_tiles, err_in, *ints)
    return pl.pallas_call(
        hand_over,
        out_shape=shapes,
        in_specs=[hbm] * 3,
        out_specs=(hbm,) * 3,
        scratch_shapes=[pltpu.VMEM(shape.shape, shape.dtype) for shape in shapes] + [dma((2, n + 2))],
    )(*results)


def solution(mesh):
    n, n_dp = mesh.shape["tensor"], mesh.shape["dp"]
    return jax.shard_map(
        functools.partial(local, n, n_dp),
        mesh=mesh,
        in_specs=(
            P("pipe", "dp", "tensor"),
            P("pipe", "dp", "tensor"),
            P("pipe", "tensor", None, None),
            P("pipe", "tensor"),
            P("pipe", "tensor"),
            P("pipe", "dp", "tensor", None, None),
            P("pipe", "dp", "tensor"),
            P("pipe", "dp", "tensor"),
            P("pipe", "dp", "tensor"),
        ),
        out_specs=(
            P("pipe", "dp", "tensor", None, None),
            P("pipe", "dp", "tensor", None, None),
            P("pipe", "dp", "tensor", None, None),
        ),
        check_vma=False,
    )
```

```python
import functools

import jax
import jax.numpy as jnp
from jax import lax
from jax.experimental import pallas as pl
from jax.experimental.pallas import tpu as pltpu
from jax.sharding import PartitionSpec as P

MESH = pl.DeviceIdType.MESH
WINDOW = 4
LAG = 3
TERM_LAG = 3
BF16, F32 = jnp.bfloat16, jnp.float32


def kernel(
    n, n_dp, x_hbm, z_hbm, w_hbm, err_hbm, cols_h, rows_h, mask_h, list_h, live_h,
    recv_o, err_o, sum_o,
    cols_s, rows_s, mask_s, list_s, live_s, xv, zv, errv, zsend, zrecv, wz, wfull, idx_out, idx_in, idx_s, gsend, grecv, eout, sbuf, sumr, sumv, part, acc, packed,
    int_sem, zl_sem, xl_sem, load_sem, ix_s, ix_r, ws_s, ws_r, wb_s, wb_r, zs_s, zs_r, gr_s, gr_r, dp_s, dp_r, pp_s, pp_r, eo_s, misc,
):
    tok, blk = zsend.shape[1], zsend.shape[2]
    rounds = n - 1
    term_lag = min(TERM_LAG, rounds - 1)
    local_blocks, hidden_blocks = xv.shape[0], zv.shape[0]
    slots = acc.shape[0]
    chunks, chunk_rows = wfull.shape[2], wfull.shape[3]
    p, d, t = lax.axis_index("pipe"), lax.axis_index("dp"), lax.axis_index("tensor")
    part_of, half = lax.rem(d, chunks), lax.div(d, chunks)
    halves = n_dp // chunks

    def offset(k):
        q = lax.rem(k + rounds - 2, rounds) + 1
        dist = n // 2 - lax.div(q, 2)
        return dist + (1 - lax.rem(q, 2)) * (n - 2 * dist)

    def carries(rank):
        return lax.rem(rank, halves) == half

    def to_of(k):
        return lax.rem(t + offset(k), n)

    def from_of(k):
        return lax.rem(t + n - offset(k), n)

    def remote(src, dst, s_sem, r_sem, where):
        return pltpu.make_async_remote_copy(
            src_ref=src, dst_ref=dst, send_sem=s_sem, recv_sem=r_sem, device_id=where, device_id_type=MESH
        )

    def z_copy(k):
        return remote(zsend.at[k], zrecv.at[k], zs_s.at[k], zs_r.at[k], {"tensor": to_of(k)})

    def idx_copy(k):
        return remote(idx_out, idx_in.at[k], ix_s.at[k], ix_r.at[k], {"tensor": to_of(k)})

    def w_copy(k):
        src = w_hbm.at[0, to_of(k), pl.ds(pl.multiple_of(part_of * chunk_rows, chunk_rows), chunk_rows)]
        return remote(src, wz.at[lax.div(t, halves)], ws_s.at[k], ws_r.at[k], {"tensor": to_of(k)})

    def w_share(i):
        return remote(
            wz, wfull.at[:, half, part_of], wb_s.at[i], wb_r.at[i], {"dp": lax.rem(d + i + 1, n_dp)}
        )

    def g_copy(k):
        return remote(gsend.at[k], grecv.at[k], gr_s.at[k], gr_r.at[k], {"tensor": from_of(k)})

    barrier = pltpu.get_barrier_semaphore()

    def greet_z(i, carry):
        pl.semaphore_signal(barrier, inc=1, device_id={"tensor": lax.rem(t + i, n)}, device_id_type=MESH)
        return carry

    def greet_dp(i, carry):
        pl.semaphore_signal(barrier, inc=1, device_id={"dp": lax.rem(d + i, n_dp)}, device_id_type=MESH)
        return carry

    lax.fori_loop(1, n, greet_z, 0)
    lax.fori_loop(1, n_dp, greet_dp, 0)
    pl.semaphore_signal(barrier, inc=1, device_id={"pipe": 1 - p}, device_id_type=MESH)

    int_loads = [
        pltpu.make_async_copy(src, dst, int_sem.at[i])
        for i, (src, dst) in enumerate(
            ((cols_h, cols_s), (rows_h, rows_s), (mask_h, mask_s), (list_h, list_s), (live_h, live_s))
        )
    ]
    for load in int_loads:
        load.start()
    z_loads = [
        pltpu.make_async_copy(z_hbm.at[0, :, pl.ds(i * blk, blk)], zv.at[i], zl_sem.at[i])
        for i in range(hidden_blocks)
    ]
    x_loads = [
        pltpu.make_async_copy(x_hbm.at[0, :, pl.ds(i * blk, blk)], xv.at[i], xl_sem.at[i])
        for i in range(local_blocks)
    ]
    err_load = pltpu.make_async_copy(err_hbm.at[0, 0], errv, load_sem.at[0])
    for load in z_loads:
        load.start()
    for load in int_loads:
        load.wait()
    lane = lax.broadcasted_iota(jnp.int32, idx_out.shape, 1)
    row = jnp.zeros(idx_out.shape, jnp.int32)
    for j in range(n):
        row = jnp.where(lane == j, rows_s[0, j], row)
    idx_out[...] = row

    def z_block(j):
        return zv[cols_s[0, j]]

    for load in z_loads:
        load.wait()

    def pick(k, carry):
        zsend[k] = z_block(to_of(k))
        return carry

    lax.fori_loop(0, min(WINDOW, rounds), pick, 0)

    own_w = pltpu.make_async_copy(
        w_hbm.at[0, t, pl.ds(pl.multiple_of(part_of * chunk_rows, chunk_rows), chunk_rows)],
        wz.at[lax.div(t, halves)],
        load_sem.at[1],
    )

    @pl.when(carries(t))
    def _():
        own_w.start()
    for load in (*x_loads, err_load):
        load.start()
    pl.semaphore_wait(barrier, n - 1 + n_dp - 1 + 1)

    def small(k, carry):
        idx_copy(k).start()

        @pl.when(carries(t))
        def _():
            w_copy(k).start()

        return carry


    def start_z(k, carry):
        z_copy(k).start()
        return carry

    lax.fori_loop(0, rounds, small, 0)
    lax.fori_loop(0, min(WINDOW, rounds), start_z, 0)
    lax.fori_loop(min(WINDOW, rounds), rounds, pick, 0)

    def weight_grad(zblk, b):
        g = lax.dot_general(xv[b], zblk, (((0,), (0,)), ((), ())), preferred_element_type=F32)
        return g * (1.0 / tok)

    def add_terms(zblk, src, b):
        w = wfull[lax.div(src, halves), lax.rem(src, halves)].reshape(blk, blk)
        product = lax.dot_general(zblk, w, (((1,), (1,)), ((), ())), preferred_element_type=F32)
        part[...] = product.astype(BF16).reshape(part.shape)
        for s in range(slots):
            r = list_s[0, 0, s]
            m = lax.div(r, local_blocks)
            term = part[m].astype(F32)
            miss = jnp.full((blk, blk), r - m * local_blocks - b, jnp.int32)
            acc[s] = acc[s] + jnp.where(miss == 0, term, 0.0)

    def dp_copy(slot, j):
        return remote(sbuf.at[slot], sumr.at[d], dp_s.at[slot], dp_r.at[d], {"dp": j})

    def err_copy(j):
        return pltpu.make_async_copy(eout.at[j], err_o.at[0, 0, j], eo_s.at[j])

    def feedback(slot, j, grads):
        total = grads + errv[j]
        keep = jnp.full((blk, blk), mask_s[0, 0, j], jnp.int32) == 1
        eout[j] = jnp.where(keep, 0.0, total)
        err_copy(j).start()
        sent = jnp.where(keep, total, 0.0).astype(BF16)
        sbuf[slot] = sent

        @pl.when(j != d)
        def _():
            dp_copy(slot, j).start()

        @pl.when(j == d)
        def _():
            sumr[d] = sent

    for load in (*x_loads, err_load):
        load.wait()
    for s in range(slots):
        acc[s] = jnp.zeros((blk, blk), F32)
    feedback(rounds, t, weight_grad(z_block(t), lax.rem(rows_s[0, t], local_blocks)))

    def got_idx(k, carry):
        idx_copy(k).wait_recv()
        return carry

    lax.fori_loop(0, rounds, got_idx, 0)
    to_smem = pltpu.make_async_copy(idx_in, idx_s, misc.at[0])
    to_smem.start()

    def got_w(k, carry):
        @pl.when(carries(from_of(k)))
        def _():
            w_copy(k).wait_recv()

        return carry

    lax.fori_loop(0, rounds, got_w, 0)

    @pl.when(carries(t))
    def _():
        own_w.wait()

    keep_w = pltpu.make_async_copy(wz, wfull.at[:, half, part_of], misc.at[1])
    keep_w.start()

    def share(i, carry):
        w_share(i).start()
        return carry

    lax.fori_loop(0, n_dp - 1, share, 0)
    to_smem.wait()
    keep_w.wait()

    def got_share(i, carry):
        w_share(i).wait_recv()
        return carry
        return carry

    def returned(k):
        g_copy(k).wait_recv()
        feedback(k, to_of(k), grecv[k].astype(F32))

    def local_of(k):
        return lax.rem(idx_s[k, 0, t], local_blocks)

    def terms(k):
        add_terms(zrecv[k], from_of(k), local_of(k))

    def one_round(k, carry):
        z_copy(k).wait_recv()

        @pl.when(k + WINDOW < rounds)
        def _():
            z_copy(k + WINDOW).start()

        gsend[k] = weight_grad(zrecv[k], local_of(k)).astype(BF16)
        g_copy(k).start()

        @pl.when(k == term_lag)
        def _():
            lax.fori_loop(0, n_dp - 1, got_share, 0)

        @pl.when(k >= term_lag)
        def _():
            terms(k - term_lag)

        @pl.when(k >= LAG)
        def _():
            returned(k - LAG)

        return carry

    lax.fori_loop(0, rounds, one_round, 0)
    lax.fori_loop(rounds - term_lag, rounds, lambda k, carry: (terms(k), carry)[1], 0)
    add_terms(z_block(t), t, lax.rem(rows_s[0, t], local_blocks))
    live = live_s[0, 0, 0]
    for s in range(slots):
        packed[s] = jnp.where(jnp.full((blk, blk), live, jnp.int32) > s, acc[s], 0.0).astype(BF16)
    over = remote(packed, recv_o.at[0, 0], pp_s.at[0], pp_r.at[0], {"pipe": 1 - p})
    over.start()
    for k in range(rounds - LAG, rounds):
        returned(k)

    def drain(k, carry):
        z_copy(k).wait_send()
        idx_copy(k).wait_send()
        g_copy(k).wait_send()

        @pl.when(carries(t))
        def _():
            w_copy(k).wait_send()

        @pl.when(to_of(k) != d)
        def _():
            dp_copy(k, to_of(k)).wait_send()

        return carry

    def drain_share(i, carry):
        w_share(i).wait_send()
        return carry

    lax.fori_loop(0, rounds, drain, 0)
    lax.fori_loop(0, n_dp - 1, drain_share, 0)

    @pl.when(t != d)
    def _():
        dp_copy(rounds, t).wait_send()

    def dp_in(i, total):
        src = lax.rem(d + i, n_dp)
        remote(sbuf.at[0], sumr.at[src], dp_s.at[0], dp_r.at[src], {"dp": src}).wait_recv()
        return total + sumr[src].astype(F32)

    sumv[...] = lax.fori_loop(1, n_dp, dp_in, sumr[d].astype(F32))
    out = pltpu.make_async_copy(sumv, sum_o.at[0, 0, 0], misc.at[2])
    out.start()

    def drain_err(j, carry):
        err_copy(j).wait()
        return carry

    lax.fori_loop(0, n, drain_err, 0)
    over.wait()
    out.wait()


def hand_over(tiles_in, err_in, sum_in, tiles_out, err_out, sum_out, tiles, err, total, sem):
    steps = [(tiles_in, tiles, tiles_out), (sum_in, total, sum_out)]
    piece = err_in.shape[2] // 4
    steps += [tuple(ref.at[0, 0, j * piece : j * piece + piece] for ref in (err_in, err, err_out)) for j in range(4)]
    arriving = [pltpu.make_async_copy(src, mid, sem.at[0, i]) for i, (src, mid, _) in enumerate(steps)]
    leaving = [pltpu.make_async_copy(mid, dst, sem.at[1, i]) for i, (_, mid, dst) in enumerate(steps)]
    for copy in arriving:
        copy.start()
    for before, after in zip(arriving, leaving):
        before.wait()
        after.start()
    for copy in leaving:
        copy.wait()


def local(n, n_dp, x_act, grad_z, weight_tiles, tile_rows, tile_cols, err_in, kept_mask, tile_list, live_count):
    tok, width = x_act.shape[1], x_act.shape[2]
    hidden = grad_z.shape[2]
    blk = weight_tiles.shape[2]
    slots = tile_list.shape[2]
    rounds = n - 1
    chunks = min(8, n_dp)
    rows = blk // chunks
    halves = n_dp // chunks
    dma = pltpu.SemaphoreType.DMA
    hbm = pl.BlockSpec(memory_space=pl.ANY)
    ints = (tile_cols, tile_rows, kept_mask, tile_list, live_count)
    shapes = (
        jax.ShapeDtypeStruct((1, 1, slots, blk, blk), BF16),
        jax.ShapeDtypeStruct((1, 1, n, blk, blk), F32),
        jax.ShapeDtypeStruct((1, 1, 1, blk, blk), F32),
    )
    results = pl.pallas_call(
        functools.partial(kernel, n, n_dp),
        out_shape=shapes,
        in_specs=[hbm] * 9,
        out_specs=(hbm, hbm, hbm),
        scratch_shapes=[pltpu.SMEM(a.shape, a.dtype) for a in ints]
        + [
            pltpu.VMEM((width // blk, tok, blk), BF16),
            pltpu.VMEM((hidden // blk, tok, blk), BF16),
            pltpu.VMEM((n, blk, blk), F32),
            pltpu.VMEM((rounds, tok, blk), BF16),
            pltpu.VMEM((rounds, tok, blk), BF16),
            pltpu.VMEM((n // halves, rows, blk), BF16),
            pltpu.VMEM((n // halves, halves, chunks, rows, blk), BF16),
            pltpu.VMEM((1, blk), jnp.int32),
            pltpu.VMEM((rounds, 1, blk), jnp.int32),
            pltpu.SMEM((rounds, 1, blk), jnp.int32),
            pltpu.VMEM((rounds, blk, blk), BF16),
            pltpu.VMEM((rounds, blk, blk), BF16),
            pltpu.VMEM((n, blk, blk), F32),
            pltpu.VMEM((n, blk, blk), BF16),
            pltpu.VMEM((n_dp, blk, blk), BF16),
            pltpu.VMEM((blk, blk), F32),
            pltpu.VMEM((tok // blk, blk, blk), BF16),
            pltpu.VMEM((slots, blk, blk), F32),
            pltpu.VMEM((slots, blk, blk), BF16),
            dma((len(ints),)), dma((hidden // blk,)), dma((width // blk,)), dma((2,)),
            dma((rounds,)), dma((rounds,)),
            dma((rounds,)), dma((rounds,)),
            dma((n_dp - 1,)), dma((n_dp - 1,)),
            dma((rounds,)), dma((rounds,)),
            dma((rounds,)), dma((rounds,)),
            dma((n,)), dma((n_dp,)),
            dma((1,)), dma((1,)),
            dma((n,)),
            dma((3,)),
        ],
        compiler_params=pltpu.CompilerParams(
            collective_id=0, has_side_effects=True, vmem_limit_bytes=56 * 2**20
        ),
        cost_estimate=pl.CostEstimate(flops=10**9, bytes_accessed=5 * 10**6, transcendentals=0),
    )(x_act, grad_z, weight_tiles, err_in, *ints)
    return pl.pallas_call(
        hand_over,
        out_shape=shapes,
        in_specs=[hbm] * 3,
        out_specs=(hbm,) * 3,
        scratch_shapes=[pltpu.VMEM(shape.shape, shape.dtype) for shape in shapes] + [dma((2, 6))],
    )(*results)


def solution(mesh):
    n, n_dp = mesh.shape["tensor"], mesh.shape["dp"]
    return jax.shard_map(
        functools.partial(local, n, n_dp),
        mesh=mesh,
        in_specs=(
            P("pipe", "dp", "tensor"),
            P("pipe", "dp", "tensor"),
            P("pipe", "tensor", None, None),
            P("pipe", "tensor"),
            P("pipe", "tensor"),
            P("pipe", "dp", "tensor", None, None),
            P("pipe", "dp", "tensor"),
            P("pipe", "dp", "tensor"),
            P("pipe", "dp", "tensor"),
        ),
        out_specs=(
            P("pipe", "dp", "tensor", None, None),
            P("pipe", "dp", "tensor", None, None),
            P("pipe", "dp", "tensor", None, None),
        ),
        check_vma=False,
    )
```

```python
import functools

import jax
import jax.numpy as jnp
from jax import lax
from jax.experimental import pallas as pl
from jax.experimental.pallas import tpu as pltpu
from jax.sharding import PartitionSpec as P

MESH = pl.DeviceIdType.MESH
WINDOW = 4
LAG = 3
TERM_LAG = 3
BF16, F32 = jnp.bfloat16, jnp.float32


def kernel(
    n, n_dp, x_hbm, z_hbm, w_hbm, err_hbm, cols_h, rows_h, mask_h, list_h, live_h,
    recv_o, err_o, sum_o,
    cols_s, rows_s, mask_s, list_s, live_s, xv, zv, errv, zsend, zrecv, wz, wfull, idx_out, idx_in, idx_s, gsend, grecv, eout, sbuf, sumr, sumv, part, acc, packed,
    int_sem, zl_sem, xl_sem, load_sem, ix_s, ix_r, ws_s, ws_r, wb_s, wb_r, zs_s, zs_r, gr_s, gr_r, dp_s, dp_r, pp_s, pp_r, eo_s, misc,
):
    tok, blk = zsend.shape[1], zsend.shape[2]
    rounds = n - 1
    term_lag = min(TERM_LAG, rounds - 1)
    local_blocks, hidden_blocks = xv.shape[0], zv.shape[0]
    slots = acc.shape[0]
    chunks, chunk_rows = wfull.shape[2], wfull.shape[3]
    p, d, t = lax.axis_index("pipe"), lax.axis_index("dp"), lax.axis_index("tensor")
    part_of, half = lax.rem(d, chunks), lax.div(d, chunks)
    halves = n_dp // chunks

    def offset(k):
        q = lax.rem(k + rounds - 2, rounds) + 1
        dist = n // 2 - lax.div(q, 2)
        return dist + (1 - lax.rem(q, 2)) * (n - 2 * dist)

    def carries(rank):
        return lax.rem(rank, halves) == half

    def to_of(k):
        return lax.rem(t + offset(k), n)

    def from_of(k):
        return lax.rem(t + n - offset(k), n)

    def remote(src, dst, s_sem, r_sem, where):
        return pltpu.make_async_remote_copy(
            src_ref=src, dst_ref=dst, send_sem=s_sem, recv_sem=r_sem, device_id=where, device_id_type=MESH
        )

    def z_copy(k):
        return remote(zsend.at[k], zrecv.at[k], zs_s.at[k], zs_r.at[k], {"tensor": to_of(k)})

    def idx_copy(k):
        return remote(idx_out, idx_in.at[k], ix_s.at[k], ix_r.at[k], {"tensor": to_of(k)})

    def w_copy(k):
        src = w_hbm.at[0, to_of(k), pl.ds(pl.multiple_of(part_of * chunk_rows, chunk_rows), chunk_rows)]
        return remote(src, wz.at[lax.div(t, halves)], ws_s.at[k], ws_r.at[k], {"tensor": to_of(k)})

    def w_share(i):
        return remote(
            wz, wfull.at[:, half, part_of], wb_s.at[i], wb_r.at[i], {"dp": lax.rem(d + i + 1, n_dp)}
        )

    def g_copy(k):
        return remote(gsend.at[k], grecv.at[k], gr_s.at[k], gr_r.at[k], {"tensor": from_of(k)})

    barrier = pltpu.get_barrier_semaphore()

    def greet_z(i, carry):
        pl.semaphore_signal(barrier, inc=1, device_id={"tensor": lax.rem(t + i, n)}, device_id_type=MESH)
        return carry

    def greet_dp(i, carry):
        pl.semaphore_signal(barrier, inc=1, device_id={"dp": lax.rem(d + i, n_dp)}, device_id_type=MESH)
        return carry

    lax.fori_loop(1, n, greet_z, 0)
    lax.fori_loop(1, n_dp, greet_dp, 0)
    pl.semaphore_signal(barrier, inc=1, device_id={"pipe": 1 - p}, device_id_type=MESH)

    int_loads = [
        pltpu.make_async_copy(src, dst, int_sem.at[i])
        for i, (src, dst) in enumerate(
            ((cols_h, cols_s), (rows_h, rows_s), (mask_h, mask_s), (list_h, list_s), (live_h, live_s))
        )
    ]
    for load in int_loads:
        load.start()
    z_loads = [
        pltpu.make_async_copy(z_hbm.at[0, :, pl.ds(i * blk, blk)], zv.at[i], zl_sem.at[i])
        for i in range(hidden_blocks)
    ]
    x_loads = [
        pltpu.make_async_copy(x_hbm.at[0, :, pl.ds(i * blk, blk)], xv.at[i], xl_sem.at[i])
        for i in range(local_blocks)
    ]
    err_load = pltpu.make_async_copy(err_hbm.at[0, 0], errv, load_sem.at[0])
    for load in z_loads:
        load.start()
    for load in int_loads:
        load.wait()
    lane = lax.broadcasted_iota(jnp.int32, idx_out.shape, 1)
    row = jnp.zeros(idx_out.shape, jnp.int32)
    for j in range(n):
        row = jnp.where(lane == j, rows_s[0, j], row)
    idx_out[...] = row

    def z_block(j):
        return zv[cols_s[0, j]]

    for load in z_loads:
        load.wait()

    def pick(k, carry):
        zsend[k] = z_block(to_of(k))
        return carry

    lax.fori_loop(0, min(WINDOW, rounds), pick, 0)

    own_w = pltpu.make_async_copy(
        w_hbm.at[0, t, pl.ds(pl.multiple_of(part_of * chunk_rows, chunk_rows), chunk_rows)],
        wz.at[lax.div(t, halves)],
        load_sem.at[1],
    )

    @pl.when(carries(t))
    def _():
        own_w.start()
    for load in (*x_loads, err_load):
        load.start()
    pl.semaphore_wait(barrier, n - 1 + n_dp - 1 + 1)

    def small(k, carry):
        idx_copy(k).start()

        @pl.when(carries(t))
        def _():
            w_copy(k).start()

        return carry


    def start_z(k, carry):
        z_copy(k).start()
        return carry

    lax.fori_loop(0, rounds, small, 0)
    lax.fori_loop(0, min(WINDOW, rounds), start_z, 0)
    lax.fori_loop(min(WINDOW, rounds), rounds, pick, 0)

    def weight_grad(zblk, b):
        g = lax.dot_general(xv[b], zblk, (((0,), (0,)), ((), ())), preferred_element_type=F32)
        return g * (1.0 / tok)

    def add_terms(zblk, src, b):
        w = wfull[lax.div(src, halves), lax.rem(src, halves)].reshape(blk, blk)
        product = lax.dot_general(zblk, w, (((1,), (1,)), ((), ())), preferred_element_type=F32)
        part[...] = product.astype(BF16).reshape(part.shape)
        for s in range(slots):
            r = list_s[0, 0, s]
            m = lax.div(r, local_blocks)
            term = part[m].astype(F32)
            miss = jnp.full((blk, blk), r - m * local_blocks - b, jnp.int32)
            acc[s] = acc[s] + jnp.where(miss == 0, term, 0.0)

    def dp_copy(slot, j):
        return remote(sbuf.at[slot], sumr.at[d], dp_s.at[slot], dp_r.at[d], {"dp": j})

    def err_copy(j):
        return pltpu.make_async_copy(eout.at[j], err_o.at[0, 0, j], eo_s.at[j])

    def feedback(slot, j, grads):
        total = grads + errv[j]
        keep = jnp.full((blk, blk), mask_s[0, 0, j], jnp.int32) == 1
        eout[j] = jnp.where(keep, 0.0, total)
        err_copy(j).start()
        sent = jnp.where(keep, total, 0.0).astype(BF16)
        sbuf[slot] = sent

        @pl.when(j != d)
        def _():
            dp_copy(slot, j).start()

        @pl.when(j == d)
        def _():
            sumr[d] = sent

    for load in (*x_loads, err_load):
        load.wait()
    for s in range(slots):
        acc[s] = jnp.zeros((blk, blk), F32)
    feedback(rounds, t, weight_grad(z_block(t), lax.rem(rows_s[0, t], local_blocks)))

    def got_idx(k, carry):
        idx_copy(k).wait_recv()
        return carry

    lax.fori_loop(0, rounds, got_idx, 0)
    to_smem = pltpu.make_async_copy(idx_in, idx_s, misc.at[0])
    to_smem.start()

    def got_w(k, carry):
        @pl.when(carries(from_of(k)))
        def _():
            w_copy(k).wait_recv()

        return carry

    lax.fori_loop(0, rounds, got_w, 0)

    @pl.when(carries(t))
    def _():
        own_w.wait()

    keep_w = pltpu.make_async_copy(wz, wfull.at[:, half, part_of], misc.at[1])
    keep_w.start()

    def share(i, carry):
        w_share(i).start()
        return carry

    lax.fori_loop(0, n_dp - 1, share, 0)
    to_smem.wait()
    keep_w.wait()

    def got_share(i, carry):
        w_share(i).wait_recv()
        return carry
        return carry

    def returned(k):
        g_copy(k).wait_recv()
        feedback(k, to_of(k), grecv[k].astype(F32))

    def local_of(k):
        return lax.rem(idx_s[k, 0, t], local_blocks)

    def terms(k):
        add_terms(zrecv[k], from_of(k), local_of(k))

    def one_round(k, carry):
        z_copy(k).wait_recv()

        @pl.when(k + WINDOW < rounds)
        def _():
            z_copy(k + WINDOW).start()

        gsend[k] = weight_grad(zrecv[k], local_of(k)).astype(BF16)
        g_copy(k).start()

        @pl.when(k >= LAG)
        def _():
            returned(k - LAG)

        @pl.when(k == term_lag)
        def _():
            lax.fori_loop(0, n_dp - 1, got_share, 0)
            add_terms(z_block(t), t, lax.rem(rows_s[0, t], local_blocks))

        @pl.when(k >= term_lag)
        def _():
            terms(k - term_lag)

        return carry

    lax.fori_loop(0, rounds, one_round, 0)
    def drain(k, carry):
        z_copy(k).wait_send()
        idx_copy(k).wait_send()
        g_copy(k).wait_send()

        @pl.when(carries(t))
        def _():
            w_copy(k).wait_send()

        return carry

    def drain_share(i, carry):
        w_share(i).wait_send()
        return carry

    for k in range(rounds - LAG, rounds - 1):
        returned(k)
    lax.fori_loop(rounds - term_lag, rounds, lambda k, carry: (terms(k), carry)[1], 0)
    live = live_s[0, 0, 0]
    for s in range(slots):
        packed[s] = jnp.where(jnp.full((blk, blk), live, jnp.int32) > s, acc[s], 0.0).astype(BF16)
    over = remote(packed, recv_o.at[0, 0], pp_s.at[0], pp_r.at[0], {"pipe": 1 - p})
    over.start()
    lax.fori_loop(0, n_dp - 1, drain_share, 0)
    lax.fori_loop(0, rounds - 2, drain, 0)
    returned(rounds - 1)
    lax.fori_loop(rounds - 2, rounds, drain, 0)

    def dp_in(i, total):
        src = lax.rem(d + i, n_dp)
        remote(sbuf.at[0], sumr.at[src], dp_s.at[0], dp_r.at[src], {"dp": src}).wait_recv()
        return total + sumr[src].astype(F32)

    sumv[...] = lax.fori_loop(1, n_dp, dp_in, sumr[d].astype(F32))
    out = pltpu.make_async_copy(sumv, sum_o.at[0, 0, 0], misc.at[2])
    out.start()

    def drain_err(j, carry):
        err_copy(j).wait()
        return carry

    def drain_dp(k, carry):
        @pl.when(to_of(k) != d)
        def _():
            dp_copy(k, to_of(k)).wait_send()

        return carry

    lax.fori_loop(0, n, drain_err, 0)
    lax.fori_loop(0, rounds, drain_dp, 0)

    @pl.when(t != d)
    def _():
        dp_copy(rounds, t).wait_send()

    over.wait()
    out.wait()


def hand_over(tiles_in, err_in, sum_in, tiles_out, err_out, sum_out, tiles, err, total, sem):
    steps = [(tiles_in, tiles, tiles_out), (sum_in, total, sum_out)]
    piece = err_in.shape[2] // 4
    steps += [tuple(ref.at[0, 0, j * piece : j * piece + piece] for ref in (err_in, err, err_out)) for j in range(4)]
    arriving = [pltpu.make_async_copy(src, mid, sem.at[0, i]) for i, (src, mid, _) in enumerate(steps)]
    leaving = [pltpu.make_async_copy(mid, dst, sem.at[1, i]) for i, (_, mid, dst) in enumerate(steps)]
    for copy in arriving:
        copy.start()
    for before, after in zip(arriving, leaving):
        before.wait()
        after.start()
    for copy in leaving:
        copy.wait()


def local(n, n_dp, x_act, grad_z, weight_tiles, tile_rows, tile_cols, err_in, kept_mask, tile_list, live_count):
    tok, width = x_act.shape[1], x_act.shape[2]
    hidden = grad_z.shape[2]
    blk = weight_tiles.shape[2]
    slots = tile_list.shape[2]
    rounds = n - 1
    chunks = min(8, n_dp)
    rows = blk // chunks
    halves = n_dp // chunks
    dma = pltpu.SemaphoreType.DMA
    hbm = pl.BlockSpec(memory_space=pl.ANY)
    ints = (tile_cols, tile_rows, kept_mask, tile_list, live_count)
    shapes = (
        jax.ShapeDtypeStruct((1, 1, slots, blk, blk), BF16),
        jax.ShapeDtypeStruct((1, 1, n, blk, blk), F32),
        jax.ShapeDtypeStruct((1, 1, 1, blk, blk), F32),
    )
    results = pl.pallas_call(
        functools.partial(kernel, n, n_dp),
        out_shape=shapes,
        in_specs=[hbm] * 9,
        out_specs=(hbm, hbm, hbm),
        scratch_shapes=[pltpu.SMEM(a.shape, a.dtype) for a in ints]
        + [
            pltpu.VMEM((width // blk, tok, blk), BF16),
            pltpu.VMEM((hidden // blk, tok, blk), BF16),
            pltpu.VMEM((n, blk, blk), F32),
            pltpu.VMEM((rounds, tok, blk), BF16),
            pltpu.VMEM((rounds, tok, blk), BF16),
            pltpu.VMEM((n // halves, rows, blk), BF16),
            pltpu.VMEM((n // halves, halves, chunks, rows, blk), BF16),
            pltpu.VMEM((1, blk), jnp.int32),
            pltpu.VMEM((rounds, 1, blk), jnp.int32),
            pltpu.SMEM((rounds, 1, blk), jnp.int32),
            pltpu.VMEM((rounds, blk, blk), BF16),
            pltpu.VMEM((rounds, blk, blk), BF16),
            pltpu.VMEM((n, blk, blk), F32),
            pltpu.VMEM((n, blk, blk), BF16),
            pltpu.VMEM((n_dp, blk, blk), BF16),
            pltpu.VMEM((blk, blk), F32),
            pltpu.VMEM((tok // blk, blk, blk), BF16),
            pltpu.VMEM((slots, blk, blk), F32),
            pltpu.VMEM((slots, blk, blk), BF16),
            dma((len(ints),)), dma((hidden // blk,)), dma((width // blk,)), dma((2,)),
            dma((rounds,)), dma((rounds,)),
            dma((rounds,)), dma((rounds,)),
            dma((n_dp - 1,)), dma((n_dp - 1,)),
            dma((rounds,)), dma((rounds,)),
            dma((rounds,)), dma((rounds,)),
            dma((n,)), dma((n_dp,)),
            dma((1,)), dma((1,)),
            dma((n,)),
            dma((3,)),
        ],
        compiler_params=pltpu.CompilerParams(
            collective_id=0, has_side_effects=True, vmem_limit_bytes=56 * 2**20
        ),
        cost_estimate=pl.CostEstimate(flops=10**9, bytes_accessed=5 * 10**6, transcendentals=0),
    )(x_act, grad_z, weight_tiles, err_in, *ints)
    return pl.pallas_call(
        hand_over,
        out_shape=shapes,
        in_specs=[hbm] * 3,
        out_specs=(hbm,) * 3,
        scratch_shapes=[pltpu.VMEM(shape.shape, shape.dtype) for shape in shapes] + [dma((2, 6))],
    )(*results)


def solution(mesh):
    n, n_dp = mesh.shape["tensor"], mesh.shape["dp"]
    return jax.shard_map(
        functools.partial(local, n, n_dp),
        mesh=mesh,
        in_specs=(
            P("pipe", "dp", "tensor"),
            P("pipe", "dp", "tensor"),
            P("pipe", "tensor", None, None),
            P("pipe", "tensor"),
            P("pipe", "tensor"),
            P("pipe", "dp", "tensor", None, None),
            P("pipe", "dp", "tensor"),
            P("pipe", "dp", "tensor"),
            P("pipe", "dp", "tensor"),
        ),
        out_specs=(
            P("pipe", "dp", "tensor", None, None),
            P("pipe", "dp", "tensor", None, None),
            P("pipe", "dp", "tensor", None, None),
        ),
        check_vma=False,
    )
```
